32 devices in a mesh: loop: 8 (over y, x, core), group: 4 (over z).
Axes of the slice: x: 2, y: 2, z: 4, core: 2. Of those that a mesh axis runs over, the one named last changes fastest.
Arguments:
- embeddings: bfloat16 [4096, 1024], P(('loop', 'group')), may hold values from -8 to 8
- partner: int32 [4096], P(('loop', 'group')), may hold values from 0 to 4095, as said below
Outputs:
- loss: float32 [], replicated
- log_norm: float32 [4096], P(('loop', 'group'))
- grad: float32 [4096, 1024], P(('loop', 'group'))
The draws below stay inside these ranges and needn't reach their ends.
Inputs may be any that keep to these rules, and one draw needn't show every extreme that they name: partner[partner[i]] = i and partner[i] != i for every view i.
All inputs are finite; a program needn't handle non-finite values.
Results may differ from the reference program's by a relative error of at most 0.0022.
Values may be sent and summed in bfloat16 or wider, within the bound.
A program may use at most 64 MiB of HBM per device.

```python
import math
import jax
import jax.numpy as jnp
from jax import lax

D = 1024
BLOCK = 512
VIEWS = 4096
N_LOOP = 8


def pair_table(key):
    order = jax.random.permutation(key, VIEWS).astype(jnp.int32)
    first = order[0::2]
    second = order[1::2]
    table = jnp.zeros((VIEWS,), jnp.int32).at[first].set(second).at[second].set(first)
    return table


def draw_partner(key, part):
    return pair_table(key)


def draw_embeddings(key, part):
    mates = pair_table(key)
    key = jax.random.fold_in(key, 7)
    key_pair, key_own = jax.random.split(key, 2)
    view_ids = jnp.arange(VIEWS, dtype=jnp.int32)
    leader = jnp.minimum(view_ids, mates)
    common = jax.random.normal(key_pair, (VIEWS, D), jnp.float32)
    single = jax.random.normal(key_own, (VIEWS, D), jnp.float32)
    values = 0.45 * common[leader] + 0.89 * single
    values = jnp.clip(values, -8.0, 8.0)
    return values.astype(jnp.bfloat16)


def setup_inputs(seed: int = 0) -> dict:
    seeds = jax.random.split(jax.random.key(seed), 3)
    embeddings = draw_embeddings(jax.random.fold_in(seeds[2], 71), 0)
    partner = draw_partner(jax.random.fold_in(seeds[2], 71), 0)
    return dict(embeddings=embeddings, partner=partner)


MASKED = -1e+30

def reference(embeddings, partner):
    scale = 1.0 / math.sqrt(D)
    all_ids = jnp.arange(VIEWS, dtype=jnp.int32)
    starts = jnp.arange(N_LOOP, dtype=jnp.int32) * BLOCK

    def scores_for(start):
        rows = lax.dynamic_slice_in_dim(embeddings, start, BLOCK, 0)
        scores = jnp.dot(rows, embeddings.T, preferred_element_type=jnp.float32) * scale
        row_ids = start + jnp.arange(BLOCK, dtype=jnp.int32)
        scores = jnp.where(row_ids[:, None] == all_ids[None, :], jnp.float32(MASKED), scores)
        mates = lax.dynamic_slice_in_dim(partner, start, BLOCK, 0)
        return (scores, mates)

    def first_pass(start):
        scores, mates = scores_for(start)
        peak = lax.optimization_barrier(jnp.max(scores, axis=1))
        norms = peak + jnp.log(lax.optimization_barrier(jnp.sum(jnp.exp(scores - peak[:, None]), axis=1)))
        positive = lax.optimization_barrier(jnp.sum(jnp.where(mates[:, None] == all_ids[None, :], scores, jnp.float32(0.0)), axis=1))
        return (norms, positive)
    norms, positive = lax.map(first_pass, starts)
    log_norm = norms.reshape(VIEWS)
    positive = positive.reshape(VIEWS)
    loss = jnp.mean(log_norm - positive)

    def second_pass(start):
        scores, mates = scores_for(start)
        own_norms = lax.dynamic_slice_in_dim(log_norm, start, BLOCK, 0)
        weights = jnp.exp(scores - own_norms[:, None]) + jnp.exp(scores - log_norm[None, :])
        weights = weights - 2.0 * (mates[:, None] == all_ids[None, :]).astype(jnp.float32)
        return jnp.dot(weights.astype(jnp.bfloat16), embeddings, preferred_element_type=jnp.float32) * scale
    grad = lax.map(second_pass, starts).reshape(VIEWS, D)
    return (loss, log_norm, grad)
```

```python
import functools
import math

import jax
import jax.numpy as jnp
from jax import lax
from jax.experimental import pallas as pl
from jax.experimental.pallas import tpu as pltpu
from jax.sharding import PartitionSpec as P

MASKED = -1e30
MESH = pl.DeviceIdType.MESH


def kernel(
    loops, groups, emb_ref, prt_ref, loss_ref, norm_ref, grad_ref,
    all_e, scores, own_col, prt_col, stats,
    z_send, x_send, y_send, c_send, line_recv, part_recv, c_recv, barrier_free_send, stat_recv,
):
    l = lax.axis_index("loop")
    g = lax.axis_index("group")
    n = loops * groups
    ys = loops // 4
    rows, width = emb_ref.shape
    scale = 1.0 / math.sqrt(width)
    c = lax.rem(l, 2)
    x = lax.rem(l // 2, 2)
    y = l // 4
    me = l * groups + g

    def quad(xx, yy):
        return yy * 2 + xx

    def block(cc, q, z):
        return (q * 2 + cc) * groups + z

    def slot(q, z):
        return q * groups + z

    mine = quad(x, y)
    other_x = quad(1 - x, y)
    other_y = [quad(x, lax.rem(y + d, ys)) for d in range(1, ys)]
    other_xy = [quad(1 - x, lax.rem(y + d, ys)) for d in range(1, ys)]

    barrier = pltpu.get_barrier_semaphore()

    def greet(k, _):
        t = lax.rem(me + k, n)
        pl.semaphore_signal(
            barrier, inc=1, device_id=(t // groups, lax.rem(t, groups)), device_id_type=MESH
        )
        return 0

    lax.fori_loop(1, n, greet, 0)
    all_e[me] = emb_ref[...]
    pl.semaphore_wait(barrier, n - 1)

    pending = []

    def send(q, z, lo, size, send_sem, recv_sem, target, when=None):
        b = block(c, q, z)

        def make():
            part = all_e.at[b, pl.ds(lo, size)]
            return pltpu.make_async_remote_copy(
                src_ref=part, dst_ref=part, send_sem=send_sem, recv_sem=recv_sem,
                device_id=target, device_id_type=MESH,
            )

        def go():
            make().start()

        def done():
            make().wait_send()

        if when is None:
            go()
        else:
            pl.when(when)(go)
        pending.append((when, done))

    def arrived(q, z, lo, size, recv_sem, cc=None):
        part = all_e.at[block(c if cc is None else cc, q, z), pl.ds(lo, size)]
        pltpu.make_async_copy(part, part, recv_sem).wait()

    def both(a, b):
        return b if a is None else jnp.logical_and(a, b)

    def when_do(cond, fn):
        if cond is None:
            fn()
        else:
            pl.when(cond)(fn)

    def sides(k):
        if k == 0:
            return [(g, None, (1, -1))]
        return [(g + k, g + k < groups, (-1,)), (g - k, g - k >= 0, (1,))]

    half = rows // 2
    small = 16

    def to_z(q, z, lo, size, recv_sem, valid, steps):
        for step in steps:
            can = (g < groups - 1) if step == 1 else (g > 0)
            send(q, z, lo, size, z_send.at[slot(q, z), 0 if step == 1 else 1], recv_sem,
                 (l, g + step), both(valid, can))

    def to_sibling(q, z, valid):
        send(q, z, 0, rows, c_send.at[slot(q, z)], c_recv.at[slot(q, z)], (l + 1 - 2 * c, g), valid)

    def to_x(q, z, lo, size, recv_sem, valid):
        send(q, z, lo, size, x_send.at[slot(q, z)], recv_sem, (l + 2 - 4 * x, g), valid)

    def to_y(q, z, lo, size, recv_sem, valid):
        for d in range(1, ys):
            send(q, z, lo, size, y_send.at[slot(q, z), d - 1], recv_sem,
                 (lax.rem(y + d, ys) * 4 + x * 2 + c, g), valid)

    def own_line(k):
        for z, valid, steps in sides(k):
            s = slot(mine, z)
            if k > 0:
                when_do(valid, lambda: arrived(mine, z, 0, rows, line_recv.at[s]))
            to_z(mine, z, 0, rows, line_recv.at[s], valid, steps)
            to_x(mine, z, 0, rows, line_recv.at[s], valid)
            to_y(mine, z, 0, rows, line_recv.at[s], valid)
            to_sibling(mine, z, valid)

    def from_x(k):
        for z, valid, _ in sides(k):
            s = slot(other_x, z)
            when_do(valid, lambda: arrived(other_x, z, 0, rows, line_recv.at[s]))
            to_y(other_x, z, 0, half if k == 0 else small, part_recv.at[s, 0], valid)
            to_sibling(other_x, z, valid)

    def from_y(k):
        for z, valid, _ in sides(k):
            for q in other_y:
                s = slot(q, z)
                when_do(valid, lambda: arrived(q, z, 0, rows, line_recv.at[s]))
                if k == 0:
                    to_x(q, z, half, rows - half, part_recv.at[s, 1], valid)
                else:
                    to_x(q, z, small, small, part_recv.at[s, 1], valid)
                to_sibling(q, z, valid)

    def from_diagonal(k):
        for z, valid, steps in sides(k):
            for q in other_xy:
                s = slot(q, z)

                def wait_parts():
                    if k == 0:
                        arrived(q, z, 0, half, part_recv.at[s, 0])
                        arrived(q, z, half, rows - half, part_recv.at[s, 1])
                    else:
                        arrived(q, z, 2 * small, rows - 2 * small, line_recv.at[s])

                when_do(valid, wait_parts)
                to_z(q, z, 2 * small, rows - 2 * small, line_recv.at[s], valid, steps)
                if k > 0:
                    def wait_rest():
                        arrived(q, z, 0, small, part_recv.at[s, 0])
                        arrived(q, z, small, small, part_recv.at[s, 1])

                    when_do(valid, wait_rest)
                to_sibling(q, z, valid)

    row_iota = lax.broadcasted_iota(jnp.int32, (rows, rows), 0)
    col_iota = lax.broadcasted_iota(jnp.int32, (rows, rows), 1)

    def score(b):
        s = lax.dot_general(
            emb_ref[...], all_e[b], (((1,), (1,)), ((), ())), preferred_element_type=jnp.float32
        ) * scale
        masked = jnp.logical_and(row_iota == col_iota, b == me)
        scores[b] = jnp.where(masked, jnp.float32(MASKED), s)

    def score_own(k):
        for z, valid, _ in sides(k):
            def run():
                def body(q, _):
                    score(block(c, q, z))
                    return 0
                lax.fori_loop(0, loops // 2, body, 0)
            when_do(valid, run)

    def score_sibling(k):
        for z, valid, _ in sides(k):
            def run():
                def body(q, _):
                    arrived(q, z, 0, rows, c_recv.at[slot(q, z)], 1 - c)
                    score(block(1 - c, q, z))
                    return 0
                lax.fori_loop(0, loops // 2, body, 0)
            when_do(valid, run)

    own_line(0)
    prt = jnp.broadcast_to(prt_ref[...].astype(jnp.float32), (rows, rows))
    prt_col[...] = prt.T.astype(jnp.int32)
    if groups > 1:
        own_line(1)
    for k in range(groups):
        from_x(k)
        from_y(k)
        if k + 2 < groups:
            own_line(k + 2)
        from_diagonal(k)
        score_own(k)
        if k > 0:
            score_sibling(k - 1)
    score_sibling(groups - 1)

    peak = lax.fori_loop(
        0, n, lambda b, m: jnp.maximum(m, scores[b]), jnp.full((rows, rows), MASKED, jnp.float32)
    )
    peak = jnp.max(peak, axis=1, keepdims=True)
    peaks = jnp.broadcast_to(peak, (rows, rows))
    mates = prt_col[...]

    def sum_up(b, carry):
        mass, pos = carry
        s = scores[b]
        mass = mass + jnp.exp(s - peaks)
        pos = pos + jnp.where(mates == col_iota + b * rows, s, jnp.float32(0.0))
        return mass, pos

    zero = jnp.zeros((rows, rows), jnp.float32)
    mass, pos = lax.fori_loop(0, n, sum_up, (zero, zero))
    norm = peak + jnp.log(jnp.sum(mass, axis=1, keepdims=True))
    term = norm - jnp.sum(pos, axis=1, keepdims=True)
    own_col[...] = jnp.broadcast_to(norm, (rows, rows))
    norm_row = own_col[...].T
    term_row = jnp.broadcast_to(term, (rows, rows)).T
    sub = lax.broadcasted_iota(jnp.int32, (8, rows), 0)
    stats[me] = jnp.where(sub == 0, norm_row[:8], term_row[:8])
    norm_ref[...] = norm_row[:1]

    def tell(k, _):
        t = lax.rem(me + k, n)
        pltpu.make_async_remote_copy(
            src_ref=stats.at[me], dst_ref=stats.at[me],
            send_sem=barrier_free_send, recv_sem=stat_recv,
            device_id=(t // groups, lax.rem(t, groups)), device_id_type=MESH,
        ).start()
        return 0

    lax.fori_loop(1, n, tell, 0)
    everyone = stats.at[pl.ds(0, n - 1)]
    pltpu.make_async_copy(everyone, everyone, stat_recv).wait()

    per = 8
    own_norm = own_col[...]
    for j in range(0, n, per):
        def weigh(b):
            s = scores[b]
            w = jnp.exp(s - own_norm) + jnp.exp(s - stats[b, 0:1, :])
            w = w - jnp.where(mates == col_iota + b * rows, jnp.float32(2.0), jnp.float32(0.0))
            return w.astype(jnp.bfloat16)

        w = jnp.concatenate([weigh(j + i) for i in range(per)], axis=1)
        e = all_e[pl.ds(j, per)].reshape(per * rows, width)
        part = jnp.dot(w, e, preferred_element_type=jnp.float32)
        if j == 0:
            grad_ref[...] = part
        elif j + per < n:
            grad_ref[...] += part
        else:
            grad_ref[...] = (grad_ref[...] + part) * scale

    loss_ref[0, 0] = jnp.sum(stats[:, 1, :]) / (n * rows)

    for when, done in pending:
        when_do(when, done)
    pltpu.make_async_copy(everyone, everyone, barrier_free_send).wait()


def solution(mesh):
    loops, groups = mesh.shape["loop"], mesh.shape["group"]
    n = loops * groups
    half = n // 2
    ys = loops // 4

    def per_device(embeddings, partner):
        rows, width = embeddings.shape
        vmem = pl.BlockSpec(memory_space=pltpu.VMEM)
        loss, norm, grad = pl.pallas_call(
            functools.partial(kernel, loops, groups),
            out_shape=(
                jax.ShapeDtypeStruct((1, 1), jnp.float32),
                jax.ShapeDtypeStruct((1, rows), jnp.float32),
                jax.ShapeDtypeStruct((rows, width), jnp.float32),
            ),
            in_specs=[vmem, vmem],
            out_specs=(pl.BlockSpec(memory_space=pltpu.SMEM), vmem, vmem),
            scratch_shapes=[
                pltpu.VMEM((n, rows, width), jnp.bfloat16),
                pltpu.VMEM((n, rows, rows), jnp.float32),
                pltpu.VMEM((rows, rows), jnp.float32),
                pltpu.VMEM((rows, rows), jnp.int32),
                pltpu.VMEM((n, 8, rows), jnp.float32),
                pltpu.SemaphoreType.DMA((half, 2)),
                pltpu.SemaphoreType.DMA((half,)),
                pltpu.SemaphoreType.DMA((half, ys - 1)),
                pltpu.SemaphoreType.DMA((half,)),
                pltpu.SemaphoreType.DMA((half,)),
                pltpu.SemaphoreType.DMA((half, 2)),
                pltpu.SemaphoreType.DMA((half,)),
                pltpu.SemaphoreType.DMA,
                pltpu.SemaphoreType.DMA,
            ],
            compiler_params=pltpu.CompilerParams(
                collective_id=0, has_side_effects=True, vmem_limit_bytes=56 * 2**20
            ),
            cost_estimate=pl.CostEstimate(
                flops=4 * n * rows * rows * width, bytes_accessed=6 * rows * width,
                transcendentals=3 * n * rows * rows,
            ),
        )(embeddings, partner.reshape(1, rows))
        return loss.reshape(()), norm.reshape(rows), grad

    placed = (P(("loop", "group"), None), P(("loop", "group")))
    return jax.shard_map(
        per_device,
        mesh=mesh,
        in_specs=placed,
        out_specs=(P(), P(("loop", "group")), P(("loop", "group"), None)),
        check_vma=False,
    )
```

```python
import functools
import math

import jax
import jax.numpy as jnp
from jax import lax
from jax.experimental import pallas as pl
from jax.experimental.pallas import tpu as pltpu
from jax.sharding import PartitionSpec as P

MASKED = -1e30
MESH = pl.DeviceIdType.MESH


def kernel(
    loops, groups, emb_ref, prt_ref, loss_ref, norm_ref, grad_ref,
    all_e, scores, shares, own_col, prt_col, peaks, mass, pos, stats,
    z_send, x_send, y_send, c_send, line_recv, part_recv, c_recv, barrier_free_send, stat_recv,
):
    l = lax.axis_index("loop")
    g = lax.axis_index("group")
    n = loops * groups
    ys = loops // 4
    rows, width = emb_ref.shape
    scale = 1.0 / math.sqrt(width)
    c = lax.rem(l, 2)
    x = lax.rem(l // 2, 2)
    y = l // 4
    me = l * groups + g

    def quad(xx, yy):
        return yy * 2 + xx

    def block(cc, q, z):
        return (q * 2 + cc) * groups + z

    def slot(q, z):
        return q * groups + z

    mine = quad(x, y)
    other_x = quad(1 - x, y)
    other_y = [quad(x, lax.rem(y + d, ys)) for d in range(1, ys)]
    other_xy = [quad(1 - x, lax.rem(y + d, ys)) for d in range(1, ys)]

    barrier = pltpu.get_barrier_semaphore()

    def greet(ll, gg):
        pl.semaphore_signal(barrier, inc=1, device_id=(ll, gg), device_id_type=MESH)

    greet(l + 1 - 2 * c, g)
    greet(l + 2 - 4 * x, g)
    for d in range(1, ys):
        greet(lax.rem(y + d, ys) * 4 + x * 2 + c, g)
    pl.when(g < groups - 1)(lambda: greet(l, g + 1))
    pl.when(g > 0)(lambda: greet(l, g - 1))
    all_e[me] = emb_ref[...]
    ends = (g < groups - 1).astype(jnp.int32) + (g > 0).astype(jnp.int32)
    pl.semaphore_wait(barrier, 1 + ys + ends)

    pending = []

    def send(q, z, lo, size, send_sem, recv_sem, target, when=None):
        b = block(c, q, z)

        def make():
            part = all_e.at[b, pl.ds(lo, size)]
            return pltpu.make_async_remote_copy(
                src_ref=part, dst_ref=part, send_sem=send_sem, recv_sem=recv_sem,
                device_id=target, device_id_type=MESH,
            )

        def go():
            make().start()

        def done():
            make().wait_send()

        if when is None:
            go()
        else:
            pl.when(when)(go)
        pending.append((when, done))

    def arrived(q, z, lo, size, recv_sem, cc=None):
        part = all_e.at[block(c if cc is None else cc, q, z), pl.ds(lo, size)]
        pltpu.make_async_copy(part, part, recv_sem).wait()

    def both(a, b):
        return b if a is None else jnp.logical_and(a, b)

    def when_do(cond, fn):
        if cond is None:
            fn()
        else:
            pl.when(cond)(fn)

    def sides(k):
        if k == 0:
            return [(g, None, (1, -1))]
        return [(g + k, g + k < groups, (-1,)), (g - k, g - k >= 0, (1,))]

    half = rows // 2

    def cuts(k):
        if k == 0:
            return half, rows
        return (16 if k % 2 else 32), 48

    def to_z(q, z, lo, size, recv_sem, valid, steps):
        for step in steps:
            can = (g < groups - 1) if step == 1 else (g > 0)
            send(q, z, lo, size, z_send.at[slot(q, z), 0 if step == 1 else 1], recv_sem,
                 (l, g + step), both(valid, can))

    def to_sibling(q, z, valid):
        send(q, z, 0, rows, c_send.at[slot(q, z)], c_recv.at[slot(q, z)], (l + 1 - 2 * c, g), valid)

    def to_x(q, z, lo, size, recv_sem, valid):
        send(q, z, lo, size, x_send.at[slot(q, z)], recv_sem, (l + 2 - 4 * x, g), valid)

    def to_y(q, z, lo, size, recv_sem, valid):
        for d in range(1, ys):
            send(q, z, lo, size, y_send.at[slot(q, z), d - 1], recv_sem,
                 (lax.rem(y + d, ys) * 4 + x * 2 + c, g), valid)

    def own_line(k, first=True, second=True):
        for z, valid, steps in sides(k):
            s = slot(mine, z)
            if first:
                if k > 0:
                    when_do(valid, lambda: arrived(mine, z, 0, rows, line_recv.at[s]))
                to_z(mine, z, 0, rows, line_recv.at[s], valid, steps)
            if second:
                to_x(mine, z, 0, rows, line_recv.at[s], valid)
                to_y(mine, z, 0, rows, line_recv.at[s], valid)
                to_sibling(mine, z, valid)

    def from_x(k):
        for z, valid, _ in sides(k):
            s = slot(other_x, z)
            when_do(valid, lambda: arrived(other_x, z, 0, rows, line_recv.at[s]))
            to_y(other_x, z, 0, cuts(k)[0], part_recv.at[s, 0], valid)
            to_sibling(other_x, z, valid)

    def from_y(k):
        lo, hi = cuts(k)
        for z, valid, _ in sides(k):
            for q in other_y:
                s = slot(q, z)
                when_do(valid, lambda: arrived(q, z, 0, rows, line_recv.at[s]))
                to_x(q, z, lo, hi - lo, part_recv.at[s, 1], valid)
                to_sibling(q, z, valid)

    def diagonal_in_plane(k):
        lo, hi = cuts(k)
        for z, valid, _ in sides(k):
            for q in other_xy:
                s = slot(q, z)

                def wait_parts():
                    arrived(q, z, 0, lo, part_recv.at[s, 0])
                    arrived(q, z, lo, hi - lo, part_recv.at[s, 1])

                when_do(valid, wait_parts)
                if k > 0:
                    to_sibling(q, z, valid)

    def diagonal_along_z(k):
        for z, valid, steps in sides(k):
            for q in other_xy:
                s = slot(q, z)
                if k > 0:
                    when_do(valid, lambda: arrived(q, z, 48, rows - 48, line_recv.at[s]))
                to_z(q, z, 48, rows - 48, line_recv.at[s], valid, steps)
                if k == 0:
                    to_sibling(q, z, valid)

    row_iota = lax.broadcasted_iota(jnp.int32, (rows, rows), 0)
    col_iota = lax.broadcasted_iota(jnp.int32, (rows, rows), 1)

    def score(b):
        s = lax.dot_general(
            emb_ref[...], all_e[b], (((1,), (1,)), ((), ())), preferred_element_type=jnp.float32
        ) * scale
        masked = jnp.logical_and(row_iota == col_iota, b == me)
        s = jnp.where(masked, jnp.float32(MASKED), s)
        scores[b] = s
        old = peaks[...]
        new = jnp.maximum(old, s)
        mass[...] = mass[...] * jnp.exp(old - new) + jnp.exp(s - new)
        peaks[...] = new
        pos[...] += jnp.where(prt_col[...] == col_iota + b * rows, s, jnp.float32(0.0))

    def score_own(k, quads=None):
        for z, valid, _ in sides(k):
            def run():
                def body(q, _):
                    score(block(c, q, z))
                    return 0
                if quads is None:
                    lax.fori_loop(0, loops // 2, body, 0)
                else:
                    for q in quads:
                        body(q, 0)
            when_do(valid, run)

    def score_sibling(k, quads=None):
        for z, valid, _ in sides(k):
            def run():
                def body(q, _):
                    arrived(q, z, 0, rows, c_recv.at[slot(q, z)], 1 - c)
                    score(block(1 - c, q, z))
                    return 0
                if quads is None:
                    lax.fori_loop(0, loops // 2, body, 0)
                else:
                    for q in quads:
                        body(q, 0)
            when_do(valid, run)

    own_line(0)
    prt = jnp.broadcast_to(prt_ref[...].astype(jnp.float32), (rows, rows))
    prt_col[...] = prt.T.astype(jnp.int32)
    peaks[...] = jnp.full((rows, rows), MASKED, jnp.float32)
    mass[...] = jnp.zeros((rows, rows), jnp.float32)
    pos[...] = jnp.zeros((rows, rows), jnp.float32)
    if groups > 1:
        own_line(1, second=False)
    from_x(0)
    from_y(0)
    diagonal_in_plane(0)
    diagonal_along_z(0)
    if groups > 1:
        own_line(1, first=False)
    if groups > 2:
        own_line(2)
    score_own(0)
    for k in range(1, groups):
        if k + 2 < groups:
            own_line(k + 2)
        diagonal_along_z(k)
        from_x(k)
        from_y(k)
        if k > 1:
            diagonal_in_plane(k - 1)
            score_own(k - 1)
        if k == 1:
            score_sibling(0)
        if k > 2:
            score_sibling(k - 2)
    last = groups - 1
    if last > 1:
        score_sibling(last - 1)
    if last > 0:
        score_own(last, (mine, other_x, *other_y))
        score_sibling(last, (mine, other_x, *other_y))
        diagonal_in_plane(last)
        score_own(last, other_xy)
        score_sibling(last, other_xy)
    else:
        score_sibling(last)

    mates = prt_col[...]
    peak = jnp.max(peaks[...], axis=1, keepdims=True)
    norm = peak + jnp.log(jnp.sum(mass[...] * jnp.exp(peaks[...] - peak), axis=1, keepdims=True))
    term = norm - jnp.sum(pos[...], axis=1, keepdims=True)
    own_col[...] = jnp.broadcast_to(norm, (rows, rows))
    norm_row = own_col[...].T
    term_row = jnp.broadcast_to(term, (rows, rows)).T
    sub = lax.broadcasted_iota(jnp.int32, (2, rows), 0)
    stats[me] = jnp.where(sub == 0, norm_row[:2], term_row[:2])
    norm_ref[...] = norm_row[:1]

    def tell(k, _):
        t = lax.rem(me + k, n)
        pltpu.make_async_remote_copy(
            src_ref=stats.at[me], dst_ref=stats.at[me],
            send_sem=barrier_free_send, recv_sem=stat_recv,
            device_id=(t // groups, lax.rem(t, groups)), device_id_type=MESH,
        ).start()
        return 0

    lax.fori_loop(1, n, tell, 0)

    own_norm = own_col[...]

    def share(b, _):
        mate = jnp.where(mates == col_iota + b * rows, jnp.float32(2.0), jnp.float32(0.0))
        shares[b] = jnp.exp(scores[b] - own_norm) - mate
        return 0

    lax.fori_loop(0, n, share, 0)
    for when, done in pending:
        when_do(when, done)
    everyone = stats.at[pl.ds(0, n - 1)]
    pltpu.make_async_copy(everyone, everyone, stat_recv).wait()

    per = 8
    for j in range(0, n, per):
        def weigh(b):
            return (shares[b] + jnp.exp(scores[b] - stats[b, 0:1, :])).astype(jnp.bfloat16)

        w = jnp.concatenate([weigh(j + i) for i in range(per)], axis=1)
        e = all_e[pl.ds(j, per)].reshape(per * rows, width)
        part = jnp.dot(w, e, preferred_element_type=jnp.float32)
        if j == 0:
            grad_ref[...] = part
        elif j + per < n:
            grad_ref[...] += part
        else:
            grad_ref[...] = (grad_ref[...] + part) * scale

    loss_ref[0, 0] = jnp.sum(stats[:, 1, :]) / (n * rows)

    pltpu.make_async_copy(everyone, everyone, barrier_free_send).wait()


def solution(mesh):
    loops, groups = mesh.shape["loop"], mesh.shape["group"]
    n = loops * groups
    half = n // 2
    ys = loops // 4

    def per_device(embeddings, partner):
        rows, width = embeddings.shape
        vmem = pl.BlockSpec(memory_space=pltpu.VMEM)
        loss, norm, grad = pl.pallas_call(
            functools.partial(kernel, loops, groups),
            out_shape=(
                jax.ShapeDtypeStruct((1, 1), jnp.float32),
                jax.ShapeDtypeStruct((1, rows), jnp.float32),
                jax.ShapeDtypeStruct((rows, width), jnp.float32),
            ),
            in_specs=[vmem, vmem],
            out_specs=(pl.BlockSpec(memory_space=pltpu.SMEM), vmem, vmem),
            scratch_shapes=[
                pltpu.VMEM((n, rows, width), jnp.bfloat16),
                pltpu.VMEM((n, rows, rows), jnp.float32),
                pltpu.VMEM((n, rows, rows), jnp.float32),
                pltpu.VMEM((rows, rows), jnp.float32),
                pltpu.VMEM((rows, rows), jnp.int32),
                pltpu.VMEM((rows, rows), jnp.float32),
                pltpu.VMEM((rows, rows), jnp.float32),
                pltpu.VMEM((rows, rows), jnp.float32),
                pltpu.VMEM((n, 2, rows), jnp.float32),
                pltpu.SemaphoreType.DMA((half, 2)),
                pltpu.SemaphoreType.DMA((half,)),
                pltpu.SemaphoreType.DMA((half, ys - 1)),
                pltpu.SemaphoreType.DMA((half,)),
                pltpu.SemaphoreType.DMA((half,)),
                pltpu.SemaphoreType.DMA((half, 2)),
                pltpu.SemaphoreType.DMA((half,)),
                pltpu.SemaphoreType.DMA,
                pltpu.SemaphoreType.DMA,
            ],
            compiler_params=pltpu.CompilerParams(
                collective_id=0, has_side_effects=True, vmem_limit_bytes=58 * 2**20
            ),
            cost_estimate=pl.CostEstimate(
                flops=4 * n * rows * rows * width, bytes_accessed=6 * rows * width,
                transcendentals=3 * n * rows * rows,
            ),
        )(embeddings, partner.reshape(1, rows))
        return loss.reshape(()), norm.reshape(rows), grad

    placed = (P(("loop", "group"), None), P(("loop", "group")))
    return jax.shard_map(
        per_device,
        mesh=mesh,
        in_specs=placed,
        out_specs=(P(), P(("loop", "group")), P(("loop", "group"), None)),
        check_vma=False,
    )
```

```python
import functools
import math

import jax
import jax.numpy as jnp
from jax import lax
from jax.experimental import pallas as pl
from jax.experimental.pallas import tpu as pltpu
from jax.sharding import PartitionSpec as P

MASKED = -1e30
MESH = pl.DeviceIdType.MESH


def kernel(
    loops, groups, emb_ref, prt_ref, loss_ref, norm_ref, grad_ref,
    all_e, scores, shares, own_col, prt_col, peaks, mass, pos, stats,
    z_send, x_send, y_send, c_send, line_recv, part_recv, c_recv, barrier_free_send, stat_recv,
):
    l = lax.axis_index("loop")
    g = lax.axis_index("group")
    n = loops * groups
    ys = loops // 4
    rows, width = emb_ref.shape
    scale = 1.0 / math.sqrt(width)
    c = lax.rem(l, 2)
    x = lax.rem(l // 2, 2)
    y = l // 4
    me = l * groups + g

    def quad(xx, yy):
        return yy * 2 + xx

    def block(cc, q, z):
        return (q * 2 + cc) * groups + z

    def slot(q, z):
        return q * groups + z

    mine = quad(x, y)
    other_x = quad(1 - x, y)
    other_y = [quad(x, lax.rem(y + d, ys)) for d in range(1, ys)]
    other_xy = [quad(1 - x, lax.rem(y + d, ys)) for d in range(1, ys)]

    barrier = pltpu.get_barrier_semaphore()

    def greet(ll, gg):
        pl.semaphore_signal(barrier, inc=1, device_id=(ll, gg), device_id_type=MESH)

    greet(l + 1 - 2 * c, g)
    greet(l + 2 - 4 * x, g)
    for d in range(1, ys):
        greet(lax.rem(y + d, ys) * 4 + x * 2 + c, g)
    pl.when(g < groups - 1)(lambda: greet(l, g + 1))
    pl.when(g > 0)(lambda: greet(l, g - 1))
    all_e[me] = emb_ref[...]
    ends = (g < groups - 1).astype(jnp.int32) + (g > 0).astype(jnp.int32)
    pl.semaphore_wait(barrier, 1 + ys + ends)

    pending = []

    def send(q, z, lo, size, send_sem, recv_sem, target, when=None):
        b = block(c, q, z)

        def make():
            part = all_e.at[b, pl.ds(lo, size)]
            return pltpu.make_async_remote_copy(
                src_ref=part, dst_ref=part, send_sem=send_sem, recv_sem=recv_sem,
                device_id=target, device_id_type=MESH,
            )

        def go():
            make().start()

        def done():
            make().wait_send()

        if when is None:
            go()
        else:
            pl.when(when)(go)
        pending.append((when, done))

    def arrived(q, z, lo, size, recv_sem, cc=None):
        part = all_e.at[block(c if cc is None else cc, q, z), pl.ds(lo, size)]
        pltpu.make_async_copy(part, part, recv_sem).wait()

    def both(a, b):
        return b if a is None else jnp.logical_and(a, b)

    def when_do(cond, fn):
        if cond is None:
            fn()
        else:
            pl.when(cond)(fn)

    def sides(k):
        if k == 0:
            return [(g, None, (1, -1))]
        return [(g + k, g + k < groups, (-1,)), (g - k, g - k >= 0, (1,))]

    half = rows // 2

    def cuts(k):
        if k == 0:
            return half, rows
        return (16 if k % 2 else 32), 48

    def to_z(q, z, lo, size, recv_sem, valid, steps):
        for step in steps:
            can = (g < groups - 1) if step == 1 else (g > 0)
            send(q, z, lo, size, z_send.at[slot(q, z), 0 if step == 1 else 1], recv_sem,
                 (l, g + step), both(valid, can))

    def to_sibling(q, z, valid):
        send(q, z, 0, rows, c_send.at[slot(q, z)], c_recv.at[slot(q, z)], (l + 1 - 2 * c, g), valid)

    def to_x(q, z, lo, size, recv_sem, valid):
        send(q, z, lo, size, x_send.at[slot(q, z)], recv_sem, (l + 2 - 4 * x, g), valid)

    def to_y(q, z, lo, size, recv_sem, valid):
        for d in range(1, ys):
            send(q, z, lo, size, y_send.at[slot(q, z), d - 1], recv_sem,
                 (lax.rem(y + d, ys) * 4 + x * 2 + c, g), valid)

    def own_line(k, first=True, second=True):
        for z, valid, steps in sides(k):
            s = slot(mine, z)
            if first:
                if k > 0:
                    when_do(valid, lambda: arrived(mine, z, 0, rows, line_recv.at[s]))
                to_z(mine, z, 0, rows, line_recv.at[s], valid, steps)
            if second:
                to_x(mine, z, 0, rows, line_recv.at[s], valid)
                to_y(mine, z, 0, rows, line_recv.at[s], valid)
                to_sibling(mine, z, valid)

    def from_x(k):
        for z, valid, _ in sides(k):
            s = slot(other_x, z)
            when_do(valid, lambda: arrived(other_x, z, 0, rows, line_recv.at[s]))
            to_y(other_x, z, 0, cuts(k)[0], part_recv.at[s, 0], valid)
            to_sibling(other_x, z, valid)

    def from_y(k):
        lo, hi = cuts(k)
        for z, valid, _ in sides(k):
            for q in other_y:
                s = slot(q, z)
                when_do(valid, lambda: arrived(q, z, 0, rows, line_recv.at[s]))
                to_x(q, z, lo, hi - lo, part_recv.at[s, 1], valid)
                to_sibling(q, z, valid)

    def diagonal_in_plane(k):
        lo, hi = cuts(k)
        for z, valid, _ in sides(k):
            for q in other_xy:
                s = slot(q, z)

                def wait_parts():
                    arrived(q, z, 0, lo, part_recv.at[s, 0])
                    arrived(q, z, lo, hi - lo, part_recv.at[s, 1])

                when_do(valid, wait_parts)
                if k > 0:
                    to_sibling(q, z, valid)

    def diagonal_along_z(k):
        for z, valid, steps in sides(k):
            for q in other_xy:
                s = slot(q, z)
                if k > 0:
                    when_do(valid, lambda: arrived(q, z, 48, rows - 48, line_recv.at[s]))
                to_z(q, z, 48, rows - 48, line_recv.at[s], valid, steps)
                if k == 0:
                    to_sibling(q, z, valid)

    row_iota = lax.broadcasted_iota(jnp.int32, (rows, rows), 0)
    col_iota = lax.broadcasted_iota(jnp.int32, (rows, rows), 1)

    def score(b):
        s = lax.dot_general(
            emb_ref[...], all_e[b], (((1,), (1,)), ((), ())), preferred_element_type=jnp.float32
        ) * scale
        masked = jnp.logical_and(row_iota == col_iota, b == me)
        s = jnp.where(masked, jnp.float32(MASKED), s)
        scores[b] = s
        old = peaks[...]
        new = jnp.maximum(old, s)
        mass[...] = mass[...] * jnp.exp(old - new) + jnp.exp(s - new)
        peaks[...] = new
        pos[...] += jnp.where(prt_col[...] == col_iota + b * rows, s, jnp.float32(0.0))

    def score_own(k, quads=None):
        for z, valid, _ in sides(k):
            def run():
                def body(q, _):
                    score(block(c, q, z))
                    return 0
                if quads is None:
                    lax.fori_loop(0, loops // 2, body, 0, unroll=4)
                else:
                    for q in quads:
                        body(q, 0)
            when_do(valid, run)

    def score_sibling(k, quads=None):
        for z, valid, _ in sides(k):
            def run():
                def body(q, _):
                    arrived(q, z, 0, rows, c_recv.at[slot(q, z)], 1 - c)
                    score(block(1 - c, q, z))
                    return 0
                if quads is None:
                    lax.fori_loop(0, loops // 2, body, 0, unroll=4)
                else:
                    for q in quads:
                        body(q, 0)
            when_do(valid, run)

    own_line(0)
    prt = jnp.broadcast_to(prt_ref[...].astype(jnp.float32), (rows, rows))
    prt_col[...] = prt.T.astype(jnp.int32)
    peaks[...] = jnp.full((rows, rows), MASKED, jnp.float32)
    mass[...] = jnp.zeros((rows, rows), jnp.float32)
    pos[...] = jnp.zeros((rows, rows), jnp.float32)
    if groups > 1:
        own_line(1, second=False)
    from_x(0)
    from_y(0)
    diagonal_in_plane(0)
    if groups > 1:
        own_line(1, first=False)
    if groups > 2:
        own_line(2)
    diagonal_along_z(0)
    score_own(0)
    for k in range(1, groups):
        if k + 2 < groups:
            own_line(k + 2)
        diagonal_along_z(k)
        from_x(k)
        from_y(k)
        if k > 1:
            diagonal_in_plane(k - 1)
            score_own(k - 1)
        if k == 1:
            score_sibling(0)
        if k > 2:
            score_sibling(k - 2)
    last = groups - 1
    if last > 1:
        score_sibling(last - 1)
    if last > 0:
        score_own(last, (mine, other_x, *other_y))
        score_sibling(last, (mine, other_x, *other_y))
        diagonal_in_plane(last)
        score_own(last, other_xy)
        score_sibling(last, other_xy)
    else:
        score_sibling(last)

    mates = prt_col[...]
    peak = jnp.max(peaks[...], axis=1, keepdims=True)
    norm = peak + jnp.log(jnp.sum(mass[...] * jnp.exp(peaks[...] - peak), axis=1, keepdims=True))
    term = norm - jnp.sum(pos[...], axis=1, keepdims=True)
    own_col[...] = jnp.broadcast_to(norm, (rows, rows))
    norm_row = own_col[...].T
    term_row = jnp.broadcast_to(term, (rows, rows)).T
    sub = lax.broadcasted_iota(jnp.int32, (2, rows), 0)
    stats[me] = jnp.where(sub == 0, norm_row[:2], term_row[:2])
    norm_ref[...] = norm_row[:1]

    def wrap(v, size):
        return jnp.where(v >= size, v - size, v)

    for dz in reversed(range(groups)):
        for dl in range(0, loops):
            if dz == 0 and dl == 0:
                continue
            pltpu.make_async_remote_copy(
                src_ref=stats.at[me], dst_ref=stats.at[me],
                send_sem=barrier_free_send, recv_sem=stat_recv,
                device_id=(wrap(l + dl, loops), wrap(g + dz, groups)), device_id_type=MESH,
            ).start()

    own_norm = own_col[...]

    def share(b, _):
        mate = jnp.where(mates == col_iota + b * rows, jnp.float32(2.0), jnp.float32(0.0))
        shares[b] = jnp.exp(scores[b] - own_norm) - mate
        return 0

    lax.fori_loop(0, n, share, 0, unroll=4)
    for when, done in pending:
        when_do(when, done)
    everyone = stats.at[pl.ds(0, n - 1)]
    pltpu.make_async_copy(everyone, everyone, stat_recv).wait()

    per = 8
    for j in range(0, n, per):
        def weigh(b):
            return (shares[b] + jnp.exp(scores[b] - stats[b, 0:1, :])).astype(jnp.bfloat16)

        w = jnp.concatenate([weigh(j + i) for i in range(per)], axis=1)
        e = all_e[pl.ds(j, per)].reshape(per * rows, width)
        part = jnp.dot(w, e, preferred_element_type=jnp.float32)
        if j == 0:
            grad_ref[...] = part
        elif j + per < n:
            grad_ref[...] += part
        else:
            grad_ref[...] = (grad_ref[...] + part) * scale

    loss_ref[0, 0] = jnp.sum(stats[:, 1, :]) / (n * rows)

    pltpu.make_async_copy(everyone, everyone, barrier_free_send).wait()


def solution(mesh):
    loops, groups = mesh.shape["loop"], mesh.shape["group"]
    n = loops * groups
    half = n // 2
    ys = loops // 4

    def per_device(embeddings, partner):
        rows, width = embeddings.shape
        vmem = pl.BlockSpec(memory_space=pltpu.VMEM)
        loss, norm, grad = pl.pallas_call(
            functools.partial(kernel, loops, groups),
            out_shape=(
                jax.ShapeDtypeStruct((1, 1), jnp.float32),
                jax.ShapeDtypeStruct((1, rows), jnp.float32),
                jax.ShapeDtypeStruct((rows, width), jnp.float32),
            ),
            in_specs=[vmem, vmem],
            out_specs=(pl.BlockSpec(memory_space=pltpu.SMEM), vmem, vmem),
            scratch_shapes=[
                pltpu.VMEM((n, rows, width), jnp.bfloat16),
                pltpu.VMEM((n, rows, rows), jnp.float32),
                pltpu.VMEM((n, rows, rows), jnp.float32),
                pltpu.VMEM((rows, rows), jnp.float32),
                pltpu.VMEM((rows, rows), jnp.int32),
                pltpu.VMEM((rows, rows), jnp.float32),
                pltpu.VMEM((rows, rows), jnp.float32),
                pltpu.VMEM((rows, rows), jnp.float32),
                pltpu.VMEM((n, 2, rows), jnp.float32),
                pltpu.SemaphoreType.DMA((half, 2)),
                pltpu.SemaphoreType.DMA((half,)),
                pltpu.SemaphoreType.DMA((half, ys - 1)),
                pltpu.SemaphoreType.DMA((half,)),
                pltpu.SemaphoreType.DMA((half,)),
                pltpu.SemaphoreType.DMA((half, 2)),
                pltpu.SemaphoreType.DMA((half,)),
                pltpu.SemaphoreType.DMA,
                pltpu.SemaphoreType.DMA,
            ],
            compiler_params=pltpu.CompilerParams(
                collective_id=0, has_side_effects=True, vmem_limit_bytes=58 * 2**20
            ),
            cost_estimate=pl.CostEstimate(
                flops=4 * n * rows * rows * width, bytes_accessed=6 * rows * width,
                transcendentals=3 * n * rows * rows,
            ),
        )(embeddings, partner.reshape(1, rows))
        return loss.reshape(()), norm.reshape(rows), grad

    placed = (P(("loop", "group"), None), P(("loop", "group")))
    return jax.shard_map(
        per_device,
        mesh=mesh,
        in_specs=placed,
        out_specs=(P(), P(("loop", "group")), P(("loop", "group"), None)),
        check_vma=False,
    )
```
